512 devices in a mesh: band: 128 (over z, y_lo, x, core), head: 4 (over y_hi).
Axes of the slice: x: 4, y: 8 (y_hi: 4, y_lo: 2; y = y_hi * 2 + y_lo), z: 8, core: 2. Of those that a mesh axis runs over, the one named last changes fastest.
Arguments:
- queries: bfloat16 [16384, 1536], P('band', 'head'), as said below
- keys: bfloat16 [16384, 1536], P('band', 'head'), as said below
- values: bfloat16 [16384, 1536], P('band', 'head'), may hold values from -6 to 6
- d_out: bfloat16 [16384, 1536], P('band', 'head'), may hold values from -6 to 6
- gain: float32 [1536], P('head'), may hold values from 0.1 to 1.9
- blocks_on: int32 [128, 4], P('band'), may hold values 0 or 1
Outputs:
- out: bfloat16 [16384, 1536], P('band', 'head')
- d_queries: bfloat16 [16384, 1536], P('band', 'head')
- d_keys: bfloat16 [16384, 1536], P('band', 'head')
- d_values: bfloat16 [16384, 1536], P('band', 'head')
The draws below stay inside these ranges and needn't reach their ends.
Inputs may be any that keep to these rules, and one draw needn't show every extreme that they name: `queries`: entries lie within -180 to 180. `keys`: entries lie within -6 to 6.
All inputs are finite; a program needn't handle non-finite values. No bound on the sum of `blocks_on` on one device may be relied on, other than what follows from the above.
Results may differ from the reference program's by a relative error of at most 0.0063.
Values may be sent and summed in bfloat16 or wider, within the bound.
A program may use at most 64 MiB of HBM per device.

```python
import jax
import jax.numpy as jnp
from jax import lax

HEADS = 12
HEAD_DIM = 128
WIDTH = 1536
TOK_DEV = 128
NOFF = 4
BLOCKS = 128
DILATION_STRIDE = 16
TOKENS = 16384


def common_keys(key):
    drawn = jax.random.normal(jax.random.fold_in(key, 11), (TOKENS, WIDTH), jnp.float32)
    return jnp.clip(drawn, -6.0, 6.0)


def draw_keys(key, part):
    return common_keys(key).astype(jnp.bfloat16)


def draw_queries(key, part):
    drawn = jnp.clip(jax.random.normal(jax.random.fold_in(key, 12), (TOKENS, WIDTH), jnp.float32), -6.0, 6.0)
    return drawn.astype(jnp.bfloat16)


def place_ends(values, key, smallest, high):
    longest = values.shape.index(max(values.shape))
    spots = []
    for shift in (0, 1):
        where = [jax.random.randint(jax.random.fold_in(key, axis), (), 0, length) for axis, length in enumerate(values.shape)]
        where[longest] = (where[longest] + shift) % values.shape[longest]
        spots.append(tuple(where))
    return values.at[spots[0]].set(smallest).at[spots[1]].set(high)


def block_levels(key, extent, pieces, smallest, high):
    factor_of = 1.0
    for dim, shards_of in pieces:
        steps = jax.random.uniform(jax.random.fold_in(jax.random.fold_in(key, 6), dim), (shards_of,), jnp.float32, smallest / len(pieces), high / len(pieces))
        factor_of = factor_of * jnp.repeat(jnp.exp(steps), extent[dim] // shards_of).reshape((-1,) + (1,) * (len(extent) - 1 - dim))
    return factor_of


def noise(own_key, extent, width, reach, shards=(), dtype=jnp.bfloat16):
    values = width * jax.random.normal(own_key, extent, jnp.float32)
    if shards:
        values = values * block_levels(own_key, extent, shards, -0.22, 0.18)
    return jnp.clip(values, -reach, reach).astype(dtype)


def setup_inputs(seed: int = 0) -> dict:
    key_list = jax.random.split(jax.random.key(seed), 7)
    queries = draw_queries(jax.random.fold_in(key_list[6], 71), 0)
    keys = draw_keys(jax.random.fold_in(key_list[6], 71), 0)
    values = noise(key_list[2], (TOKENS, WIDTH), 1.0, 6.0, ((0, 128), (1, 4)))
    d_out = noise(key_list[3], (TOKENS, WIDTH), 1.0, 6.0, ((0, 128), (1, 4)))
    gain = jnp.clip(1.0 + 0.18 * jax.random.normal(key_list[4], (WIDTH,), jnp.float32), 0.1, 1.9)
    blocks_on = place_ends((jax.random.randint(key_list[5], (BLOCKS, NOFF), 0, 4) < 3).astype(jnp.int32), jax.random.fold_in(key_list[5], 1), 0, 1)
    return {"queries": queries, "keys": keys, "values": values, "d_out": d_out, "gain": gain, "blocks_on": blocks_on}


NEG = -1e+30
EPS = 1e-06

def reference(queries, keys, values, d_out, gain, blocks_on):
    f32 = jnp.float32
    scaling = HEAD_DIM ** (-0.5)
    block_offsets = jnp.array([0, -2 * DILATION_STRIDE, -DILATION_STRIDE, DILATION_STRIDE, 2 * DILATION_STRIDE], jnp.int32)
    allowed = jnp.concatenate([jnp.ones((BLOCKS, 1), jnp.int32), blocks_on], axis=1)
    shape4 = (BLOCKS, TOK_DEV, HEADS, HEAD_DIM)
    query4 = queries.reshape(shape4)
    key4 = keys.reshape(shape4)
    value4 = values.reshape(shape4)

    def block_scores(b):
        target = b + block_offsets
        inside = (target >= 0) & (target < BLOCKS)
        usable = inside & (allowed[b] == 1)
        target = jnp.clip(target, 0, BLOCKS - 1).astype(jnp.int32)
        key_rows = key4[target].reshape(5 * TOK_DEV, HEADS, HEAD_DIM)
        value_rows = value4[target].reshape(5 * TOK_DEV, HEADS, HEAD_DIM)
        score = jnp.einsum('qhe,khe->hqk', query4[b].astype(f32), key_rows.astype(f32)) * scaling
        column = jnp.repeat(usable, TOK_DEV)
        return (jnp.where(column[None, None, :], score, NEG), key_rows, value_rows)

    def forward_pass(b):
        score, key_rows, value_rows = block_scores(b)
        peak = lax.optimization_barrier(jnp.max(score, axis=2))
        expo = jnp.exp(score - peak[:, :, None])
        total = lax.optimization_barrier(jnp.sum(expo, axis=2))
        weight_probs = (expo / total[:, :, None]).astype(jnp.bfloat16)
        result = jnp.einsum('hqk,khe->qhe', weight_probs.astype(f32), value_rows.astype(f32))
        return (result.astype(jnp.bfloat16), peak, total)
    attention, peaks, totals = lax.map(forward_pass, jnp.arange(BLOCKS))
    attention_wide = attention.reshape(TOKENS, WIDTH).astype(f32)
    inverse = lax.rsqrt(lax.optimization_barrier(jnp.mean(attention_wide * attention_wide, axis=1)) + EPS)
    out = (attention_wide * inverse[:, None] * gain).astype(jnp.bfloat16)
    gradient_pass = d_out.astype(f32) * gain
    along = lax.optimization_barrier(jnp.sum(gradient_pass * attention_wide, axis=1))
    d_attn = (inverse[:, None] * gradient_pass - attention_wide * inverse[:, None] ** 3 * along[:, None] / WIDTH).astype(jnp.bfloat16)
    attention_grad_4d = d_attn.reshape(shape4)
    deltas = lax.optimization_barrier(jnp.sum(attention_grad_4d.astype(f32) * attention.astype(f32), axis=3))
    deltas = jnp.transpose(deltas, (0, 2, 1))

    def grad_queries(b):
        score, key_rows, value_rows = block_scores(b)
        probs = jnp.exp(score - peaks[b][:, :, None]) / totals[b][:, :, None]
        d_weights = jnp.einsum('qhe,khe->hqk', attention_grad_4d[b].astype(f32), value_rows.astype(f32))
        d_score = (probs * (d_weights - deltas[b][:, :, None])).astype(jnp.bfloat16)
        result = jnp.einsum('hqk,khe->qhe', d_score.astype(f32), key_rows.astype(f32)) * scaling
        return result.astype(jnp.bfloat16)

    def grad_keys(c):
        own_keys = key4[c].astype(f32)
        own_values = value4[c].astype(f32)
        key_sum = jnp.zeros((TOK_DEV, HEADS, HEAD_DIM), f32)
        value_sum = jnp.zeros((TOK_DEV, HEADS, HEAD_DIM), f32)
        for slot_index in range(5):
            source = c - block_offsets[slot_index]
            inside = (source >= 0) & (source < BLOCKS)
            source = jnp.clip(source, 0, BLOCKS - 1).astype(jnp.int32)
            usable = inside & (allowed[source, slot_index] == 1)
            far_queries = query4[source].astype(f32)
            far_grad = attention_grad_4d[source].astype(f32)
            score = jnp.einsum('qhe,khe->hqk', far_queries, own_keys) * scaling
            probs = jnp.exp(score - peaks[source][:, :, None]) / totals[source][:, :, None]
            probs = jnp.where(usable, probs, 0.0)
            d_weights = jnp.einsum('qhe,khe->hqk', far_grad, own_values)
            d_score = (probs * (d_weights - deltas[source][:, :, None])).astype(jnp.bfloat16)
            key_part = jnp.einsum('hqk,qhe->khe', d_score.astype(f32), far_queries) * scaling
            value_part = jnp.einsum('hqk,qhe->khe', probs.astype(jnp.bfloat16).astype(f32), far_grad)
            if slot_index > 0:
                key_part = lax.optimization_barrier(key_part.astype(jnp.bfloat16)).astype(f32)
                value_part = lax.optimization_barrier(value_part.astype(jnp.bfloat16)).astype(f32)
            key_sum = key_sum + key_part
            value_sum = value_sum + value_part
        return (key_sum.astype(jnp.bfloat16), value_sum.astype(jnp.bfloat16))
    d_queries = lax.map(grad_queries, jnp.arange(BLOCKS)).reshape(TOKENS, WIDTH)
    d_keys, d_values = lax.map(grad_keys, jnp.arange(BLOCKS))
    return (out, d_queries, d_keys.reshape(TOKENS, WIDTH), d_values.reshape(TOKENS, WIDTH))
```

```python
import functools

import jax
import jax.numpy as jnp
from jax import lax
from jax.experimental import pallas as pl
from jax.experimental.pallas import tpu as pltpu
from jax.sharding import PartitionSpec as P

D = 128
NEG = -1e30
EPS = 1e-06
VMEM = 32 * 1024 * 1024
MESH = pl.DeviceIdType.MESH
BF16 = jnp.bfloat16
F32 = jnp.float32

SLOT_OFFSET = (0, -1, 1, -2, 2)
COLUMN = {-2: 0, -1: 1, 1: 2, 2: 3}
NEAR = {1: 1, -1: 2}
FAR = {1: 3, -1: 4}


def nt(left, right):
    return lax.dot_general(left, right, (((1,), (1,)), ((), ())), preferred_element_type=F32)


def nn(left, right):
    return jnp.dot(left, right, preferred_element_type=F32)


def kernel(
    heads,
    spacing,
    steps,
    peers,
    q_hbm,
    k_hbm,
    v_hbm,
    do_hbm,
    gain_hbm,
    on_hbm,
    out_ref,
    dq_ref,
    dk_ref,
    dv_ref,
    kb,
    vb,
    qb,
    ab,
    dob,
    gain_ref,
    on_ref,
    attn,
    score,
    probs,
    score_t,
    probs_t,
    dk_acc,
    dv_acc,
    st1,
    st2,
    sums,
    send_sem,
    recv_sem,
    local_sem,
):
    me = lax.axis_index("band")
    hd = lax.axis_index("head")
    z = me // spacing
    width = heads * D
    full_width = width * peers
    scaling = D ** (-0.5)

    def inside(offset):
        return (z + offset >= 0) & (z + offset < steps)

    def slot(index):
        return pl.ds(index * D, D)

    def cols(h):
        return slice(h * D, (h + 1) * D)

    barrier = pltpu.get_barrier_semaphore()
    expected = jnp.int32(peers - 1)
    for d in (1, -1):

        @pl.when(inside(d))
        def _():
            pl.semaphore_signal(barrier, 1, device_id=(me + d * spacing, hd), device_id_type=MESH)

        expected = expected + inside(d).astype(jnp.int32)
    for p in range(1, peers):
        pl.semaphore_signal(barrier, 1, device_id=(me, lax.rem(hd + p, peers)), device_id_type=MESH)
    local = []

    def fetch(src, dst):
        copy = pltpu.make_async_copy(src, dst, local_sem.at[len(local)])
        copy.start()
        local.append(copy)

    fetch(on_hbm, on_ref)
    for h in range(heads):
        fetch(q_hbm.at[:, cols(h)], qb.at[h, slot(0)])
        fetch(k_hbm.at[:, cols(h)], kb.at[h, slot(0)])
    for h in range(heads):
        fetch(v_hbm.at[:, cols(h)], vb.at[h, slot(0)])
    fetch(gain_hbm, gain_ref)
    for h in range(heads):
        fetch(do_hbm.at[:, cols(h)], dob.at[h])

    pl.semaphore_wait(barrier, expected)

    used = [0]
    sent = []

    def remote(src, dst, device, condition):
        index = used[0]
        used[0] += 1
        copy = pltpu.make_async_remote_copy(
            src, dst, send_sem.at[index], recv_sem.at[index], device_id=device, device_id_type=MESH
        )
        sent.append((copy, condition))
        return copy

    def first_step(src, dst_of, d):
        copy = remote(src, dst_of(NEAR[d]), (me + d * spacing, hd), inside(d))
        pl.when(inside(d))(copy.start)
        return copy

    def second_step(first, dst_of, d):
        copy = remote(dst_of(NEAR[d]), dst_of(FAR[d]), (me + d * spacing, hd), inside(d) & inside(-d))

        @pl.when(inside(-d))
        def _():
            first.wait_recv()
            pl.when(inside(d))(copy.start)

        return copy

    def arrived(second, d):
        pl.when(inside(-2 * d))(second.wait_recv)

    def rows_of(buffer, h):
        return lambda index: buffer.at[h, slot(index)]

    def tile_of(buffer):
        return lambda index: buffer.at[index]

    both = (1, -1)
    k1 = {(h, d): first_step(k_hbm.at[:, cols(h)], rows_of(kb, h), d) for h in range(heads) for d in both}
    v1 = {(h, d): first_step(v_hbm.at[:, cols(h)], rows_of(vb, h), d) for h in range(heads) for d in both}

    for d in both:
        for index, away in ((NEAR[d], -d), (FAR[d], -2 * d)):

            @pl.when(jnp.logical_not(inside(away)))
            def _():
                for buffer in (kb, vb, qb, ab):
                    for h in range(heads):
                        buffer[h, slot(index)] = jnp.zeros((D, D), BF16)
                st1[index] = jnp.zeros(st1.shape[1:], F32)
                st2[index] = jnp.zeros(st2.shape[1:], F32)

    for copy in local:
        copy.wait()
    allowed = {}
    for offset, column in COLUMN.items():
        allowed[offset] = inside(offset) & (on_ref[0, column] == 1)
    factor = {0: scaling}
    shift = {0: 0.0}
    for offset in COLUMN:
        factor[offset] = jnp.where(allowed[offset], scaling, 0.0).astype(F32)
        shift[offset] = jnp.where(allowed[offset], 0.0, NEG).astype(F32)


    def compute_scores(h, index):
        offset = SLOT_OFFSET[index]
        raw = nt(qb[h, slot(0)], kb[h, slot(index)])
        score[h, :, slot(index)] = raw * factor[offset] + shift[offset]

    for h in range(heads):
        compute_scores(h, 0)
    k2 = {}
    for h in range(heads):
        for d in both:
            k2[h, d] = second_step(k1[h, d], rows_of(kb, h), d)
        for d in both:
            compute_scores(h, NEAR[d])
    v2 = {}
    for h in range(heads):
        for d in both:
            v2[h, d] = second_step(v1[h, d], rows_of(vb, h), d)
    q1 = {(h, d): first_step(q_hbm.at[:, cols(h)], rows_of(qb, h), d) for h in range(heads) for d in both}

    lane = lax.broadcasted_iota(jnp.int32, (D, D), 1)

    def as_rows(columns):
        packed = jnp.zeros((D, D), F32)
        for i, column in enumerate(columns):
            packed = jnp.where(lane == i, column, packed)
        return packed.T

    peaks, inverses = [], []
    for h in range(heads):
        for d in both:
            arrived(k2[h, d], d)
        for d in both:
            compute_scores(h, FAR[d])
        pieces = [score[h, :, slot(i)] for i in range(5)]
        top = functools.reduce(jnp.maximum, pieces)
        peak = jnp.max(top, axis=1, keepdims=True)
        exponents = [jnp.exp(piece - peak) for piece in pieces]
        total = jnp.sum(functools.reduce(jnp.add, exponents), axis=1, keepdims=True)
        inverse_total = 1.0 / total
        for i in range(5):
            weight = exponents[i] * inverse_total
            score[h, :, slot(i)] = weight
            probs[h, :, slot(i)] = weight.astype(BF16)
        peaks.append(peak)
        inverses.append(inverse_total)
    st1[0] = as_rows(peaks + inverses + [-shift[offset] for offset in COLUMN])[0:16]
    s1 = {d: first_step(st1.at[0], tile_of(st1), d) for d in both}

    near_rows = 3 * D
    partial = [nn(probs[h, :, 0:near_rows], vb[h, 0:near_rows]) for h in range(heads)]
    sums_g, sums_a = [], []
    for h in range(heads):
        for d in both:
            arrived(v2[h, d], d)
        value = partial[h] + nn(probs[h, :, near_rows:], vb[h, near_rows:])
        attn[h] = value.astype(BF16)
        wide = attn[h].astype(F32)
        gradient = dob[h].astype(F32) * gain_ref[cols(h)][None, :]
        sums_g.append(jnp.sum(gradient * wide, axis=1, keepdims=True))
        sums_a.append(jnp.sum(wide * wide, axis=1, keepdims=True))
    sums[0] = as_rows([functools.reduce(jnp.add, sums_g), functools.reduce(jnp.add, sums_a)])[0:8]
    exchanged = []
    for p in range(1, peers):
        copy = remote(sums.at[0], sums.at[p], (me, lax.rem(hd + p, peers)), True)
        copy.start()
        exchanged.append(copy)

    s2 = {d: second_step(s1[d], tile_of(st1), d) for d in both}
    q2 = {}
    for h in range(heads):
        for d in both:
            q2[h, d] = second_step(q1[h, d], rows_of(qb, h), d)

    def weights_back(h, index):
        offset = SLOT_OFFSET[index]
        peak = st1[index, h : h + 1]
        if offset:
            row = 2 * heads + COLUMN[-offset]
            peak = peak + st1[index, row : row + 1]
        raw = nt(kb[h, slot(0)], qb[h, slot(index)]) * scaling
        weight = jnp.exp(raw - peak) * st1[index, heads + h : heads + h + 1]
        score_t[h, :, slot(index)] = weight
        probs_t[h, :, slot(index)] = weight.astype(BF16)

    for h in range(heads):
        for index in range(3):
            weights_back(h, index)

    for copy in exchanged:
        copy.wait_recv()
    all_rows = functools.reduce(jnp.add, [sums[p] for p in range(peers)])
    along = all_rows[0:1]
    square = all_rows[1:2]
    inverse = lax.rsqrt(square / full_width + EPS)
    coefficient = inverse * inverse * inverse * along / full_width
    sublane = lax.broadcasted_iota(jnp.int32, (D, D), 0)
    columns = jnp.where(sublane == 0, inverse, coefficient).T
    inverse_col = columns[:, 0:1]
    coefficient_col = columns[:, 1:2]
    a1 = {}
    for h in range(heads):
        gradient = dob[h].astype(F32) * gain_ref[cols(h)][None, :]
        wide = attn[h].astype(F32)
        ab[h, slot(0)] = (inverse_col * gradient - wide * coefficient_col).astype(BF16)
        for d in both:
            a1[h, d] = first_step(ab.at[h, slot(0)], rows_of(ab, h), d)
    deltas = [
        jnp.sum(ab[h, slot(0)].astype(F32) * attn[h].astype(F32), axis=1, keepdims=True) for h in range(heads)
    ]
    st2[0] = as_rows(deltas)[0:8]
    e1 = {d: first_step(st2.at[0], tile_of(st2), d) for d in both}
    for h in range(heads):
        out_ref[:, cols(h)] = (attn[h].astype(F32) * inverse_col * gain_ref[cols(h)][None, :]).astype(BF16)

    def query_gradient(h):
        d_weights = nt(ab[h, slot(0)], vb[h])
        d_score = (score[h] * (d_weights - deltas[h])).astype(BF16)
        dq_ref[:, cols(h)] = (nn(d_score, kb[h]) * scaling).astype(BF16)

    def key_gradients(h, low, high):
        rows = slice(low * D, high * D)
        delta = jnp.concatenate([st2[i, h : h + 1] for i in range(low, high)], axis=1)
        value_part = nn(probs_t[h, :, rows], ab[h, rows])
        d_weights = nt(vb[h, slot(0)], ab[h, rows])
        d_score = (score_t[h, :, rows] * (d_weights - delta)).astype(BF16)
        return nn(d_score, qb[h, rows]), value_part

    for h in range(heads):
        query_gradient(h)
    for h in range(heads):
        dk_acc[h], dv_acc[h] = key_gradients(h, 0, 1)
    for d in both:
        arrived(s2[d], d)
    for h in range(heads):
        for d in both:
            arrived(q2[h, d], d)
        for d in both:
            weights_back(h, FAR[d])
    e2 = {d: second_step(e1[d], tile_of(st2), d) for d in both}
    a2 = {}
    for h in range(heads):
        for d in both:
            a2[h, d] = second_step(a1[h, d], rows_of(ab, h), d)
    for h in range(heads):
        key_part, value_part = key_gradients(h, 1, 3)
        dk_acc[h] += key_part
        dv_acc[h] += value_part
    for d in both:
        arrived(e2[d], d)
    for h in range(heads):
        for d in both:
            arrived(a2[h, d], d)
        key_part, value_part = key_gradients(h, 3, 5)
        dk_ref[:, cols(h)] = ((dk_acc[h] + key_part) * scaling).astype(BF16)
        dv_ref[:, cols(h)] = (dv_acc[h] + value_part).astype(BF16)
    for copy, condition in sent:
        if condition is True:
            copy.wait_send()
        else:
            pl.when(condition)(copy.wait_send)


def hand_on(*refs):
    *refs, sem = refs
    copies = []
    for i, (src, dst) in enumerate(zip(refs[: len(refs) // 2], refs[len(refs) // 2 :])):
        copies.append(pltpu.make_async_copy(src, dst, sem.at[i]))
        copies[-1].start()
    for copy in copies:
        copy.wait()


def local(queries, keys, values, d_out, gain, blocks_on):
    rows, width = queries.shape
    heads = width // D
    spacing = lax.axis_size("band") // 8
    peers = lax.axis_size("head")
    block = jax.ShapeDtypeStruct((rows, width), BF16)
    anywhere = pl.BlockSpec(memory_space=pl.ANY)
    vmem = pl.BlockSpec(memory_space=pltpu.VMEM)
    copies = 2 * 2 * 4 * heads + 8 + peers - 1
    results = pl.pallas_call(
        functools.partial(kernel, heads, spacing, 8, peers),
        out_shape=[block] * 4,
        in_specs=[anywhere] * 6,
        out_specs=[vmem] * 4,
        scratch_shapes=[pltpu.VMEM((heads, 5 * D, D), BF16)] * 4
        + [
            pltpu.VMEM((heads, D, D), BF16),
            pltpu.VMEM((width,), F32),
            pltpu.SMEM((1, 4), jnp.int32),
            pltpu.VMEM((heads, D, D), BF16),
            pltpu.VMEM((heads, D, 5 * D), F32),
            pltpu.VMEM((heads, D, 5 * D), BF16),
            pltpu.VMEM((heads, D, 5 * D), F32),
            pltpu.VMEM((heads, D, 5 * D), BF16),
            pltpu.VMEM((heads, D, D), F32),
            pltpu.VMEM((heads, D, D), F32),
            pltpu.VMEM((5, 16, D), F32),
            pltpu.VMEM((5, 8, D), F32),
            pltpu.VMEM((peers, 8, D), F32),
            pltpu.SemaphoreType.DMA((copies,)),
            pltpu.SemaphoreType.DMA((copies,)),
            pltpu.SemaphoreType.DMA((4 * heads + 2,)),
        ],
        compiler_params=pltpu.CompilerParams(
            collective_id=0, has_side_effects=True, vmem_limit_bytes=VMEM
        ),
        cost_estimate=pl.CostEstimate(flops=505_000_000, bytes_accessed=800_000, transcendentals=500_000),
        name="attention",
    )(*[pltpu.with_memory_space_constraint(x, pltpu.HBM) for x in (queries, keys, values, d_out, gain, blocks_on)])
    passed = pl.pallas_call(
        hand_on,
        out_shape=[block] * 4,
        in_specs=[vmem] * 4,
        out_specs=[anywhere] * 4,
        scratch_shapes=[pltpu.SemaphoreType.DMA((4,))],
        compiler_params=pltpu.CompilerParams(vmem_limit_bytes=8 * 1024 * 1024),
        name="hand_on",
    )(*results)
    return tuple(passed)


def solution(mesh):
    in_specs = (
        P("band", "head"),
        P("band", "head"),
        P("band", "head"),
        P("band", "head"),
        P("head"),
        P("band", None),
    )
    out_specs = (P("band", "head"), P("band", "head"), P("band", "head"), P("band", "head"))
    return jax.shard_map(local, mesh=mesh, in_specs=in_specs, out_specs=out_specs, check_vma=False)
```

```python
import functools

import jax
import jax.numpy as jnp
from jax import lax
from jax.experimental import pallas as pl
from jax.experimental.pallas import tpu as pltpu
from jax.sharding import PartitionSpec as P

D = 128
NEG = -1e30
EPS = 1e-06
VMEM = 32 * 1024 * 1024
MESH = pl.DeviceIdType.MESH
BF16 = jnp.bfloat16
F32 = jnp.float32

SLOT_OFFSET = (0, -1, 1, -2, 2)
COLUMN = {-2: 0, -1: 1, 1: 2, 2: 3}
NEAR = {1: 1, -1: 2}
FAR = {1: 3, -1: 4}


def nt(left, right):
    return lax.dot_general(left, right, (((1,), (1,)), ((), ())), preferred_element_type=F32)


def nn(left, right):
    return jnp.dot(left, right, preferred_element_type=F32)


def kernel(
    heads,
    spacing,
    steps,
    peers,
    q_hbm,
    k_hbm,
    v_hbm,
    do_hbm,
    gain_hbm,
    on_hbm,
    out_ref,
    dq_ref,
    dk_ref,
    dv_ref,
    kb,
    vb,
    qb,
    ab,
    dob,
    gain_ref,
    on_ref,
    attn,
    score,
    probs,
    score_t,
    probs_t,
    dk_acc,
    dv_acc,
    st1,
    st2,
    sums,
    send_sem,
    recv_sem,
    local_sem,
):
    me = lax.axis_index("band")
    hd = lax.axis_index("head")
    z = me // spacing
    core = lax.rem(me, 2)
    width = heads * D
    full_width = width * peers
    scaling = D ** (-0.5)

    def inside(offset):
        return (z + offset >= 0) & (z + offset < steps)

    def slot(index):
        return pl.ds(index * D, D)

    def cols(h):
        return slice(h * D, (h + 1) * D)

    barrier = pltpu.get_barrier_semaphore()
    expected = jnp.int32(peers - 1)
    for d in COLUMN:

        @pl.when(inside(d))
        def _():
            pl.semaphore_signal(barrier, 1, device_id=(me + d * spacing, hd), device_id_type=MESH)

        expected = expected + inside(d).astype(jnp.int32)
    for p in range(1, peers):
        pl.semaphore_signal(barrier, 1, device_id=(me, lax.rem(hd + p, peers)), device_id_type=MESH)
    local = []

    def fetch(src, dst):
        copy = pltpu.make_async_copy(src, dst, local_sem.at[len(local)])
        copy.start()
        local.append(copy)

    fetch(on_hbm, on_ref)
    for h in range(heads):
        fetch(q_hbm.at[:, cols(h)], qb.at[h, slot(0)])
        fetch(k_hbm.at[:, cols(h)], kb.at[h, slot(0)])
    for h in range(heads):
        fetch(v_hbm.at[:, cols(h)], vb.at[h, slot(0)])
    fetch(gain_hbm, gain_ref)
    for h in range(heads):
        fetch(do_hbm.at[:, cols(h)], dob.at[h])

    pl.semaphore_wait(barrier, expected)

    used = [0]
    sent = []

    def remote(src, dst, device, condition):
        index = used[0]
        used[0] += 1
        copy = pltpu.make_async_remote_copy(
            src, dst, send_sem.at[index], recv_sem.at[index], device_id=device, device_id_type=MESH
        )
        sent.append((copy, condition))
        return copy

    def first_step(src, dst_of, d, also=True):
        copy = remote(src, dst_of(NEAR[d]), (me + d * spacing, hd), inside(d))
        pl.when(inside(d) & also)(copy.start)
        return copy

    def second_step(first, dst_of, d):
        copy = remote(dst_of(NEAR[d]), dst_of(FAR[d]), (me + d * spacing, hd), inside(d) & inside(-d))

        @pl.when(inside(-d))
        def _():
            first.wait_recv()
            pl.when(inside(d))(copy.start)

        return copy

    def straight(src, dst_of, d):
        copy = remote(src, dst_of(FAR[d]), (me + 2 * d * spacing, hd), inside(2 * d))
        pl.when(inside(2 * d))(copy.start)
        return copy

    def near_arrived(first, d):
        pl.when(inside(-d))(first.wait_recv)

    def arrived(second, d):
        pl.when(inside(-2 * d))(second.wait_recv)

    def rows_of(buffer, h):
        return lambda index: buffer.at[h, slot(index)]

    def tile_of(buffer):
        return lambda index: buffer.at[index]

    both = (1, -1)
    k1 = {(h, d): first_step(k_hbm.at[:, cols(h)], rows_of(kb, h), d) for h in range(heads) for d in both}
    v1 = {(h, d): first_step(v_hbm.at[:, cols(h)], rows_of(vb, h), d, core != 1) for h in range(heads) for d in both}

    for d in both:
        for index, away in ((NEAR[d], -d), (FAR[d], -2 * d)):

            @pl.when(jnp.logical_not(inside(away)))
            def _():
                for buffer in (kb, vb, qb, ab):
                    for h in range(heads):
                        buffer[h, slot(index)] = jnp.zeros((D, D), BF16)
                st1[index] = jnp.zeros(st1.shape[1:], F32)
                st2[index] = jnp.zeros(st2.shape[1:], F32)

    for copy in local:
        copy.wait()
    allowed = {}
    for offset, column in COLUMN.items():
        allowed[offset] = inside(offset) & (on_ref[0, column] == 1)
    factor = {0: scaling}
    shift = {0: 0.0}
    for offset in COLUMN:
        factor[offset] = jnp.where(allowed[offset], scaling, 0.0).astype(F32)
        shift[offset] = jnp.where(allowed[offset], 0.0, NEG).astype(F32)


    def compute_scores(h, index):
        offset = SLOT_OFFSET[index]
        raw = nt(qb[h, slot(0)], kb[h, slot(index)])
        score[h, :, slot(index)] = raw * factor[offset] + shift[offset]

    for h in range(heads):
        compute_scores(h, 0)
    k2 = {}
    for h in range(heads):
        for d in both:
            k2[h, d] = second_step(k1[h, d], rows_of(kb, h), d)
        for d in both:
            compute_scores(h, NEAR[d])
    for h in range(heads):
        for d in both:
            pl.when(inside(d) & (core == 1))(v1[h, d].start)
    v2 = {}
    for h in range(heads):
        for d in both:
            v2[h, d] = second_step(v1[h, d], rows_of(vb, h), d)
    q1 = {(h, d): first_step(q_hbm.at[:, cols(h)], rows_of(qb, h), d, core != 1) for h in range(heads) for d in both}

    lane = lax.broadcasted_iota(jnp.int32, (D, D), 1)

    def as_rows(columns):
        packed = jnp.zeros((D, D), F32)
        for i, column in enumerate(columns):
            packed = jnp.where(lane == i, column, packed)
        return packed.T

    peaks, inverses = [], []
    for h in range(heads):
        for d in both:
            arrived(k2[h, d], d)
        for d in both:
            compute_scores(h, FAR[d])
        pieces = [score[h, :, slot(i)] for i in range(5)]
        top = functools.reduce(jnp.maximum, pieces)
        peak = jnp.max(top, axis=1, keepdims=True)
        exponents = [jnp.exp(piece - peak) for piece in pieces]
        total = jnp.sum(functools.reduce(jnp.add, exponents), axis=1, keepdims=True)
        inverse_total = 1.0 / total
        for i in range(5):
            weight = exponents[i] * inverse_total
            score[h, :, slot(i)] = weight
            probs[h, :, slot(i)] = weight.astype(BF16)
        peaks.append(peak)
        inverses.append(inverse_total)
    for h in range(heads):
        for d in both:
            pl.when(inside(d) & (core == 1))(q1[h, d].start)
    st1[0] = as_rows(peaks + inverses + [-shift[offset] for offset in COLUMN])[0:16]
    s1 = {d: first_step(st1.at[0], tile_of(st1), d) for d in both}
    s2 = {d: straight(st1.at[0], tile_of(st1), d) for d in both}

    near_rows = 3 * D
    partial = [nn(probs[h, :, 0:near_rows], vb[h, 0:near_rows]) for h in range(heads)]
    sums_g, sums_a = [], []
    for h in range(heads):
        for d in both:
            arrived(v2[h, d], d)
        value = partial[h] + nn(probs[h, :, near_rows:], vb[h, near_rows:])
        attn[h] = value.astype(BF16)
        wide = attn[h].astype(F32)
        gradient = dob[h].astype(F32) * gain_ref[cols(h)][None, :]
        sums_g.append(jnp.sum(gradient * wide, axis=1, keepdims=True))
        sums_a.append(jnp.sum(wide * wide, axis=1, keepdims=True))
    sums[0] = as_rows([functools.reduce(jnp.add, sums_g), functools.reduce(jnp.add, sums_a)])[0:8]
    exchanged = []
    for p in range(1, peers):
        copy = remote(sums.at[0], sums.at[p], (me, lax.rem(hd + p, peers)), True)
        copy.start()
        exchanged.append(copy)

    for d in both:
        near_arrived(s1[d], d)
    q2 = {}
    for h in range(heads):
        for d in both:
            q2[h, d] = second_step(q1[h, d], rows_of(qb, h), d)

    def weights_back(h, index):
        offset = SLOT_OFFSET[index]
        peak = st1[index, h : h + 1]
        if offset:
            row = 2 * heads + COLUMN[-offset]
            peak = peak + st1[index, row : row + 1]
        raw = nt(kb[h, slot(0)], qb[h, slot(index)]) * scaling
        weight = jnp.exp(raw - peak) * st1[index, heads + h : heads + h + 1]
        score_t[h, :, slot(index)] = weight
        probs_t[h, :, slot(index)] = weight.astype(BF16)

    for h in range(heads):
        for index in range(3):
            weights_back(h, index)

    for copy in exchanged:
        copy.wait_recv()
    all_rows = functools.reduce(jnp.add, [sums[p] for p in range(peers)])
    along = all_rows[0:1]
    square = all_rows[1:2]
    inverse = lax.rsqrt(square / full_width + EPS)
    coefficient = inverse * inverse * inverse * along / full_width
    sublane = lax.broadcasted_iota(jnp.int32, (D, D), 0)
    columns = jnp.where(sublane == 0, inverse, coefficient).T
    inverse_col = columns[:, 0:1]
    coefficient_col = columns[:, 1:2]
    a1 = {}
    for h in range(heads):
        gradient = dob[h].astype(F32) * gain_ref[cols(h)][None, :]
        wide = attn[h].astype(F32)
        ab[h, slot(0)] = (inverse_col * gradient - wide * coefficient_col).astype(BF16)
        for d in both:
            a1[h, d] = first_step(ab.at[h, slot(0)], rows_of(ab, h), d)
    deltas = [
        jnp.sum(ab[h, slot(0)].astype(F32) * attn[h].astype(F32), axis=1, keepdims=True) for h in range(heads)
    ]
    st2[0] = as_rows(deltas)[0:8]
    e1 = {d: first_step(st2.at[0], tile_of(st2), d) for d in both}
    e2 = {d: straight(st2.at[0], tile_of(st2), d) for d in both}
    a2 = {}
    for h in range(heads):
        out_ref[:, cols(h)] = (attn[h].astype(F32) * inverse_col * gain_ref[cols(h)][None, :]).astype(BF16)

    def query_gradient(h):
        d_weights = nt(ab[h, slot(0)], vb[h])
        d_score = (score[h] * (d_weights - deltas[h])).astype(BF16)
        dq_ref[:, cols(h)] = (nn(d_score, kb[h]) * scaling).astype(BF16)

    def key_gradients(h, low, high):
        rows = slice(low * D, high * D)
        delta = jnp.concatenate([st2[i, h : h + 1] for i in range(low, high)], axis=1)
        value_part = nn(probs_t[h, :, rows], ab[h, rows])
        d_weights = nt(vb[h, slot(0)], ab[h, rows])
        d_score = (score_t[h, :, rows] * (d_weights - delta)).astype(BF16)
        return nn(d_score, qb[h, rows]), value_part

    for h in range(heads):
        query_gradient(h)
    for h in range(heads):
        dk_acc[h], dv_acc[h] = key_gradients(h, 0, 1)
    for d in both:
        arrived(s2[d], d)
    for h in range(heads):
        for d in both:
            arrived(q2[h, d], d)
        for d in both:
            weights_back(h, FAR[d])
    for h in range(heads):
        for d in both:
            a2[h, d] = second_step(a1[h, d], rows_of(ab, h), d)
    for d in both:
        near_arrived(e1[d], d)
    for h in range(heads):
        key_part, value_part = key_gradients(h, 1, 3)
        dk_acc[h] += key_part
        dv_acc[h] += value_part
    for d in both:
        arrived(e2[d], d)
    for h in range(heads):
        for d in both:
            arrived(a2[h, d], d)
        key_part, value_part = key_gradients(h, 3, 5)
        dk_ref[:, cols(h)] = ((dk_acc[h] + key_part) * scaling).astype(BF16)
        dv_ref[:, cols(h)] = (dv_acc[h] + value_part).astype(BF16)
    for copy, condition in sent:
        if condition is True:
            copy.wait_send()
        else:
            pl.when(condition)(copy.wait_send)


def hand_on(*refs):
    *refs, sem = refs
    copies = []
    for i, (src, dst) in enumerate(zip(refs[: len(refs) // 2], refs[len(refs) // 2 :])):
        copies.append(pltpu.make_async_copy(src, dst, sem.at[i]))
        copies[-1].start()
    for copy in copies:
        copy.wait()


def local(queries, keys, values, d_out, gain, blocks_on):
    rows, width = queries.shape
    heads = width // D
    spacing = lax.axis_size("band") // 8
    peers = lax.axis_size("head")
    block = jax.ShapeDtypeStruct((rows, width), BF16)
    anywhere = pl.BlockSpec(memory_space=pl.ANY)
    vmem = pl.BlockSpec(memory_space=pltpu.VMEM)
    copies = 2 * 2 * 4 * heads + 8 + peers - 1
    results = pl.pallas_call(
        functools.partial(kernel, heads, spacing, 8, peers),
        out_shape=[block] * 4,
        in_specs=[anywhere] * 6,
        out_specs=[vmem] * 4,
        scratch_shapes=[pltpu.VMEM((heads, 5 * D, D), BF16)] * 4
        + [
            pltpu.VMEM((heads, D, D), BF16),
            pltpu.VMEM((width,), F32),
            pltpu.SMEM((1, 4), jnp.int32),
            pltpu.VMEM((heads, D, D), BF16),
            pltpu.VMEM((heads, D, 5 * D), F32),
            pltpu.VMEM((heads, D, 5 * D), BF16),
            pltpu.VMEM((heads, D, 5 * D), F32),
            pltpu.VMEM((heads, D, 5 * D), BF16),
            pltpu.VMEM((heads, D, D), F32),
            pltpu.VMEM((heads, D, D), F32),
            pltpu.VMEM((5, 16, D), F32),
            pltpu.VMEM((5, 8, D), F32),
            pltpu.VMEM((peers, 8, D), F32),
            pltpu.SemaphoreType.DMA((copies,)),
            pltpu.SemaphoreType.DMA((copies,)),
            pltpu.SemaphoreType.DMA((4 * heads + 2,)),
        ],
        compiler_params=pltpu.CompilerParams(
            collective_id=0, has_side_effects=True, vmem_limit_bytes=VMEM
        ),
        cost_estimate=pl.CostEstimate(flops=505_000_000, bytes_accessed=800_000, transcendentals=500_000),
        name="attention",
    )(*[pltpu.with_memory_space_constraint(x, pltpu.HBM) for x in (queries, keys, values, d_out, gain, blocks_on)])
    passed = pl.pallas_call(
        hand_on,
        out_shape=[block] * 4,
        in_specs=[vmem] * 4,
        out_specs=[anywhere] * 4,
        scratch_shapes=[pltpu.SemaphoreType.DMA((4,))],
        compiler_params=pltpu.CompilerParams(vmem_limit_bytes=8 * 1024 * 1024),
        name="hand_on",
    )(*results)
    return tuple(passed)


def solution(mesh):
    in_specs = (
        P("band", "head"),
        P("band", "head"),
        P("band", "head"),
        P("band", "head"),
        P("head"),
        P("band", None),
    )
    out_specs = (P("band", "head"), P("band", "head"), P("band", "head"), P("band", "head"))
    return jax.shard_map(local, mesh=mesh, in_specs=in_specs, out_specs=out_specs, check_vma=False)
```

```python
import functools

import jax
import jax.numpy as jnp
from jax import lax
from jax.experimental import pallas as pl
from jax.experimental.pallas import tpu as pltpu
from jax.sharding import PartitionSpec as P

D = 128
NEG = -1e30
EPS = 1e-06
VMEM = 32 * 1024 * 1024
MESH = pl.DeviceIdType.MESH
BF16 = jnp.bfloat16
F32 = jnp.float32

SLOT_OFFSET = (0, -1, 1, -2, 2)
COLUMN = {-2: 0, -1: 1, 1: 2, 2: 3}
NEAR = {1: 1, -1: 2}
FAR = {1: 3, -1: 4}


def nt(left, right):
    return lax.dot_general(left, right, (((1,), (1,)), ((), ())), preferred_element_type=F32)


def nn(left, right):
    return jnp.dot(left, right, preferred_element_type=F32)


def kernel(
    heads,
    spacing,
    steps,
    peers,
    q_hbm,
    k_hbm,
    v_hbm,
    do_hbm,
    gain_hbm,
    on_hbm,
    out_ref,
    dq_ref,
    dk_ref,
    dv_ref,
    kb,
    vb,
    qb,
    ab,
    dob,
    gain_ref,
    on_ref,
    grad,
    attn,
    score,
    probs,
    score_t,
    probs_t,
    dk_acc,
    dv_acc,
    st1,
    st2,
    sums,
    send_sem,
    recv_sem,
    local_sem,
):
    me = lax.axis_index("band")
    hd = lax.axis_index("head")
    z = me // spacing
    core = lax.rem(me, 2)
    width = heads * D
    full_width = width * peers
    scaling = D ** (-0.5)

    def inside(offset):
        return (z + offset >= 0) & (z + offset < steps)

    def slot(index):
        return pl.ds(index * D, D)

    def cols(h):
        return slice(h * D, (h + 1) * D)

    barrier = pltpu.get_barrier_semaphore()
    expected = jnp.int32(peers - 1)
    for d in COLUMN:

        @pl.when(inside(d))
        def _():
            pl.semaphore_signal(barrier, 1, device_id=(me + d * spacing, hd), device_id_type=MESH)

        expected = expected + inside(d).astype(jnp.int32)
    for p in range(1, peers):
        pl.semaphore_signal(barrier, 1, device_id=(me, lax.rem(hd + p, peers)), device_id_type=MESH)
    local = []

    def fetch(src, dst):
        copy = pltpu.make_async_copy(src, dst, local_sem.at[len(local)])
        copy.start()
        local.append(copy)

    fetch(on_hbm, on_ref)
    for h in range(heads):
        fetch(q_hbm.at[:, cols(h)], qb.at[h, slot(0)])
        fetch(k_hbm.at[:, cols(h)], kb.at[h, slot(0)])
    for h in range(heads):
        fetch(v_hbm.at[:, cols(h)], vb.at[h, slot(0)])
    fetch(gain_hbm, gain_ref)
    for h in range(heads):
        fetch(do_hbm.at[:, cols(h)], dob.at[h])

    pl.semaphore_wait(barrier, expected)

    used = [0]
    sent = []

    def remote(src, dst, device, condition):
        index = used[0]
        used[0] += 1
        copy = pltpu.make_async_remote_copy(
            src, dst, send_sem.at[index], recv_sem.at[index], device_id=device, device_id_type=MESH
        )
        sent.append((copy, condition))
        return copy

    def first_step(src, dst_of, d, also=True):
        copy = remote(src, dst_of(NEAR[d]), (me + d * spacing, hd), inside(d))
        pl.when(inside(d) & also)(copy.start)
        return copy

    def second_step(first, dst_of, d):
        copy = remote(dst_of(NEAR[d]), dst_of(FAR[d]), (me + d * spacing, hd), inside(d) & inside(-d))

        @pl.when(inside(-d))
        def _():
            first.wait_recv()
            pl.when(inside(d))(copy.start)

        return copy

    def straight(src, dst_of, d):
        copy = remote(src, dst_of(FAR[d]), (me + 2 * d * spacing, hd), inside(2 * d))
        pl.when(inside(2 * d))(copy.start)
        return copy

    def near_arrived(first, d):
        pl.when(inside(-d))(first.wait_recv)

    def arrived(second, d):
        pl.when(inside(-2 * d))(second.wait_recv)

    def rows_of(buffer, h):
        return lambda index: buffer.at[h, slot(index)]

    def tile_of(buffer):
        return lambda index: buffer.at[index]

    both = (1, -1)
    k1 = {(h, d): first_step(k_hbm.at[:, cols(h)], rows_of(kb, h), d) for h in range(heads) for d in both}
    v1 = {(h, d): first_step(v_hbm.at[:, cols(h)], rows_of(vb, h), d, core != 1) for h in range(heads) for d in both}

    for d in both:
        for index, away in ((NEAR[d], -d), (FAR[d], -2 * d)):

            @pl.when(jnp.logical_not(inside(away)))
            def _():
                for buffer in (kb, vb, qb, ab):
                    for h in range(heads):
                        buffer[h, slot(index)] = jnp.zeros((D, D), BF16)
                st1[index] = jnp.zeros(st1.shape[1:], F32)
                st2[index] = jnp.zeros(st2.shape[1:], F32)

    for copy in local:
        copy.wait()
    allowed = {}
    for offset, column in COLUMN.items():
        allowed[offset] = inside(offset) & (on_ref[0, column] == 1)
    factor = {0: scaling}
    shift = {0: 0.0}
    for offset in COLUMN:
        factor[offset] = jnp.where(allowed[offset], scaling, 0.0).astype(F32)
        shift[offset] = jnp.where(allowed[offset], 0.0, NEG).astype(F32)


    def compute_scores(h, index):
        offset = SLOT_OFFSET[index]
        raw = nt(qb[h, slot(0)], kb[h, slot(index)])
        score[h, :, slot(index)] = raw * factor[offset] + shift[offset]

    for h in range(heads):
        compute_scores(h, 0)
    k2 = {}
    for h in range(heads):
        for d in both:
            k2[h, d] = second_step(k1[h, d], rows_of(kb, h), d)
        for d in both:
            compute_scores(h, NEAR[d])
    for h in range(heads):
        for d in both:
            pl.when(inside(d) & (core == 1))(v1[h, d].start)
    v2 = {}
    for h in range(heads):
        for d in both:
            v2[h, d] = second_step(v1[h, d], rows_of(vb, h), d)
    q1 = {(h, d): first_step(q_hbm.at[:, cols(h)], rows_of(qb, h), d, core != 1) for h in range(heads) for d in both}

    sums[0] = jnp.zeros(sums.shape[1:], F32)
    lane = lax.broadcasted_iota(jnp.int32, (D, D), 1)

    def as_rows(columns):
        packed = jnp.zeros((D, D), F32)
        for i, column in enumerate(columns):
            packed = jnp.where(lane == i, column, packed)
        return packed.T

    peaks, inverses = [], []
    for h in range(heads):
        for d in both:
            arrived(k2[h, d], d)
        for d in both:
            compute_scores(h, FAR[d])
        pieces = [score[h, :, slot(i)] for i in range(5)]
        top = functools.reduce(jnp.maximum, pieces)
        peak = jnp.max(top, axis=1, keepdims=True)
        exponents = [jnp.exp(piece - peak) for piece in pieces]
        total = jnp.sum(functools.reduce(jnp.add, exponents), axis=1, keepdims=True)
        inverse_total = 1.0 / total
        for i in range(5):
            weight = exponents[i] * inverse_total
            score[h, :, slot(i)] = weight
            probs[h, :, slot(i)] = weight.astype(BF16)
        peaks.append(peak)
        inverses.append(inverse_total)
    for h in range(heads):
        for d in both:
            pl.when(inside(d) & (core == 1))(q1[h, d].start)
    st1[0] = as_rows(peaks + inverses + [-shift[offset] for offset in COLUMN])[0:16]
    s1 = {d: first_step(st1.at[0], tile_of(st1), d) for d in both}
    s2 = {d: straight(st1.at[0], tile_of(st1), d) for d in both}

    near_rows = 3 * D
    partial = [nn(probs[h, :, 0:near_rows], vb[h, 0:near_rows]) for h in range(heads)]
    for h in range(heads):
        grad[h] = dob[h].astype(F32) * gain_ref[cols(h)][None, :]
    sum_g = jnp.zeros((D, D), F32)
    sum_a = jnp.zeros((D, D), F32)
    for h in range(heads):
        for d in both:
            arrived(v2[h, d], d)
        value = partial[h] + nn(probs[h, :, near_rows:], vb[h, near_rows:])
        attn[h] = value.astype(BF16)
        wide = attn[h].astype(F32)
        sum_g += grad[h] * wide
        sum_a += wide * wide
    sums[0, 0:1] = jnp.sum(sum_g.T, axis=0, keepdims=True)
    sums[0, 1:2] = jnp.sum(sum_a.T, axis=0, keepdims=True)
    exchanged = []
    for p in range(1, peers):
        copy = remote(sums.at[0], sums.at[p], (me, lax.rem(hd + p, peers)), True)
        copy.start()
        exchanged.append(copy)

    for d in both:
        near_arrived(s1[d], d)
    q2 = {}
    for h in range(heads):
        for d in both:
            q2[h, d] = second_step(q1[h, d], rows_of(qb, h), d)

    def weights_back(h, index):
        offset = SLOT_OFFSET[index]
        peak = st1[index, h : h + 1]
        if offset:
            row = 2 * heads + COLUMN[-offset]
            peak = peak + st1[index, row : row + 1]
        raw = nt(kb[h, slot(0)], qb[h, slot(index)]) * scaling
        weight = jnp.exp(raw - peak) * st1[index, heads + h : heads + h + 1]
        score_t[h, :, slot(index)] = weight
        probs_t[h, :, slot(index)] = weight.astype(BF16)

    for h in range(heads):
        for index in range(3):
            weights_back(h, index)

    for copy in exchanged:
        copy.wait_recv()
    all_rows = functools.reduce(jnp.add, [sums[p] for p in range(peers)])
    along = all_rows[0:1]
    square = all_rows[1:2]
    inverse = lax.rsqrt(square / full_width + EPS)
    coefficient = inverse * inverse * inverse * along / full_width
    sublane = lax.broadcasted_iota(jnp.int32, (D, D), 0)
    columns = jnp.where(sublane == 0, inverse, coefficient).T
    inverse_col = columns[:, 0:1]
    coefficient_col = columns[:, 1:2]
    a1 = {}
    for h in range(heads):
        gradient = grad[h]
        wide = attn[h].astype(F32)
        ab[h, slot(0)] = (inverse_col * gradient - wide * coefficient_col).astype(BF16)
        for d in both:
            a1[h, d] = first_step(ab.at[h, slot(0)], rows_of(ab, h), d)
    deltas = [
        jnp.sum(ab[h, slot(0)].astype(F32) * attn[h].astype(F32), axis=1, keepdims=True) for h in range(heads)
    ]
    st2[0] = as_rows(deltas)[0:8]
    e1 = {d: first_step(st2.at[0], tile_of(st2), d) for d in both}
    e2 = {d: straight(st2.at[0], tile_of(st2), d) for d in both}
    a2 = {}
    for h in range(heads):
        out_ref[:, cols(h)] = (attn[h].astype(F32) * inverse_col * gain_ref[cols(h)][None, :]).astype(BF16)

    def query_gradient(h):
        d_weights = nt(ab[h, slot(0)], vb[h])
        d_score = (score[h] * (d_weights - deltas[h])).astype(BF16)
        dq_ref[:, cols(h)] = (nn(d_score, kb[h]) * scaling).astype(BF16)

    def key_gradients(h, low, high):
        rows = slice(low * D, high * D)
        delta = jnp.concatenate([st2[i, h : h + 1] for i in range(low, high)], axis=1)
        value_part = nn(probs_t[h, :, rows], ab[h, rows])
        d_weights = nt(vb[h, slot(0)], ab[h, rows])
        d_score = (score_t[h, :, rows] * (d_weights - delta)).astype(BF16)
        return nn(d_score, qb[h, rows]), value_part

    for h in range(heads):
        query_gradient(h)
    for h in range(heads):
        dk_acc[h], dv_acc[h] = key_gradients(h, 0, 1)
    for d in both:
        arrived(s2[d], d)
    for h in range(heads):
        for d in both:
            arrived(q2[h, d], d)
        for d in both:
            weights_back(h, FAR[d])
    for h in range(heads):
        for d in both:
            a2[h, d] = second_step(a1[h, d], rows_of(ab, h), d)
    for d in both:
        near_arrived(e1[d], d)
    for h in range(heads):
        key_part, value_part = key_gradients(h, 1, 3)
        dk_acc[h] += key_part
        dv_acc[h] += value_part
    for d in both:
        arrived(e2[d], d)
    for h in range(heads):
        for d in both:
            arrived(a2[h, d], d)
        key_part, value_part = key_gradients(h, 3, 5)
        dk_ref[:, cols(h)] = ((dk_acc[h] + key_part) * scaling).astype(BF16)
        dv_ref[:, cols(h)] = (dv_acc[h] + value_part).astype(BF16)
    for copy, condition in sent:
        if condition is True:
            copy.wait_send()
        else:
            pl.when(condition)(copy.wait_send)


def hand_on(*refs):
    *refs, sem = refs
    copies = []
    for i, (src, dst) in enumerate(zip(refs[: len(refs) // 2], refs[len(refs) // 2 :])):
        copies.append(pltpu.make_async_copy(src, dst, sem.at[i]))
        copies[-1].start()
    for copy in copies:
        copy.wait()


def local(queries, keys, values, d_out, gain, blocks_on):
    rows, width = queries.shape
    heads = width // D
    spacing = lax.axis_size("band") // 8
    peers = lax.axis_size("head")
    block = jax.ShapeDtypeStruct((rows, width), BF16)
    anywhere = pl.BlockSpec(memory_space=pl.ANY)
    vmem = pl.BlockSpec(memory_space=pltpu.VMEM)
    copies = 2 * 2 * 4 * heads + 8 + peers - 1
    results = pl.pallas_call(
        functools.partial(kernel, heads, spacing, 8, peers),
        out_shape=[block] * 4,
        in_specs=[anywhere] * 6,
        out_specs=[vmem] * 4,
        scratch_shapes=[pltpu.VMEM((heads, 5 * D, D), BF16)] * 4
        + [
            pltpu.VMEM((heads, D, D), BF16),
            pltpu.VMEM((width,), F32),
            pltpu.SMEM((1, 4), jnp.int32),
            pltpu.VMEM((heads, D, D), F32),
            pltpu.VMEM((heads, D, D), BF16),
            pltpu.VMEM((heads, D, 5 * D), F32),
            pltpu.VMEM((heads, D, 5 * D), BF16),
            pltpu.VMEM((heads, D, 5 * D), F32),
            pltpu.VMEM((heads, D, 5 * D), BF16),
            pltpu.VMEM((heads, D, D), F32),
            pltpu.VMEM((heads, D, D), F32),
            pltpu.VMEM((5, 16, D), F32),
            pltpu.VMEM((5, 8, D), F32),
            pltpu.VMEM((peers, 8, D), F32),
            pltpu.SemaphoreType.DMA((copies,)),
            pltpu.SemaphoreType.DMA((copies,)),
            pltpu.SemaphoreType.DMA((4 * heads + 2,)),
        ],
        compiler_params=pltpu.CompilerParams(
            collective_id=0, has_side_effects=True, vmem_limit_bytes=VMEM
        ),
        cost_estimate=pl.CostEstimate(flops=505_000_000, bytes_accessed=800_000, transcendentals=500_000),
        name="attention",
    )(*[pltpu.with_memory_space_constraint(x, pltpu.HBM) for x in (queries, keys, values, d_out, gain, blocks_on)])
    passed = pl.pallas_call(
        hand_on,
        out_shape=[block] * 4,
        in_specs=[vmem] * 4,
        out_specs=[anywhere] * 4,
        scratch_shapes=[pltpu.SemaphoreType.DMA((4,))],
        compiler_params=pltpu.CompilerParams(vmem_limit_bytes=8 * 1024 * 1024),
        name="hand_on",
    )(*results)
    return tuple(passed)


def solution(mesh):
    in_specs = (
        P("band", "head"),
        P("band", "head"),
        P("band", "head"),
        P("band", "head"),
        P("head"),
        P("band", None),
    )
    out_specs = (P("band", "head"), P("band", "head"), P("band", "head"), P("band", "head"))
    return jax.shard_map(local, mesh=mesh, in_specs=in_specs, out_specs=out_specs, check_vma=False)
```

```python
import functools

import jax
import jax.numpy as jnp
from jax import lax
from jax.experimental import pallas as pl
from jax.experimental.pallas import tpu as pltpu
from jax.sharding import PartitionSpec as P

D = 128
NEG = -1e30
EPS = 1e-06
VMEM = 32 * 1024 * 1024
MESH = pl.DeviceIdType.MESH
BF16 = jnp.bfloat16
F32 = jnp.float32

SLOT_OFFSET = (0, -1, 1, -2, 2)
COLUMN = {-2: 0, -1: 1, 1: 2, 2: 3}
NEAR = {1: 1, -1: 2}
FAR = {1: 3, -1: 4}


def nt(left, right):
    return lax.dot_general(left, right, (((1,), (1,)), ((), ())), preferred_element_type=F32)


def nn(left, right):
    return jnp.dot(left, right, preferred_element_type=F32)


def kernel(
    heads,
    spacing,
    steps,
    peers,
    q_hbm,
    k_hbm,
    v_hbm,
    do_hbm,
    gain_hbm,
    on_hbm,
    out_ref,
    dq_ref,
    dk_ref,
    dv_ref,
    kb,
    vb,
    qb,
    ab,
    dob,
    gain_ref,
    on_ref,
    attn,
    score,
    probs,
    score_t,
    probs_t,
    dk_acc,
    dv_acc,
    st1,
    st2,
    sums,
    send_sem,
    recv_sem,
    local_sem,
):
    me = lax.axis_index("band")
    hd = lax.axis_index("head")
    z = me // spacing
    core = lax.rem(me, 2)
    width = heads * D
    full_width = width * peers
    scaling = D ** (-0.5)

    def inside(offset):
        return (z + offset >= 0) & (z + offset < steps)

    def slot(index):
        return pl.ds(index * D, D)

    def cols(h):
        return slice(h * D, (h + 1) * D)

    barrier = pltpu.get_barrier_semaphore()
    expected = jnp.int32(peers - 1)
    for d in COLUMN:

        @pl.when(inside(d))
        def _():
            pl.semaphore_signal(barrier, 1, device_id=(me + d * spacing, hd), device_id_type=MESH)

        expected = expected + inside(d).astype(jnp.int32)
    for p in range(1, peers):
        pl.semaphore_signal(barrier, 1, device_id=(me, lax.rem(hd + p, peers)), device_id_type=MESH)
    local = []

    def fetch(src, dst):
        copy = pltpu.make_async_copy(src, dst, local_sem.at[len(local)])
        copy.start()
        local.append(copy)

    fetch(on_hbm, on_ref)
    for h in range(heads):
        fetch(q_hbm.at[:, cols(h)], qb.at[h, slot(0)])
        fetch(k_hbm.at[:, cols(h)], kb.at[h, slot(0)])
    for h in range(heads):
        fetch(v_hbm.at[:, cols(h)], vb.at[h, slot(0)])
    fetch(gain_hbm, gain_ref)
    for h in range(heads):
        fetch(do_hbm.at[:, cols(h)], dob.at[h])

    pl.semaphore_wait(barrier, expected)

    used = [0]
    sent = []

    def remote(src, dst, device, condition):
        index = used[0]
        used[0] += 1
        copy = pltpu.make_async_remote_copy(
            src, dst, send_sem.at[index], recv_sem.at[index], device_id=device, device_id_type=MESH
        )
        sent.append((copy, condition))
        return copy

    def first_step(src, dst_of, d, also=True):
        copy = remote(src, dst_of(NEAR[d]), (me + d * spacing, hd), inside(d))
        pl.when(inside(d) & also)(copy.start)
        return copy

    def second_step(first, dst_of, d):
        copy = remote(dst_of(NEAR[d]), dst_of(FAR[d]), (me + d * spacing, hd), inside(d) & inside(-d))

        @pl.when(inside(-d))
        def _():
            first.wait_recv()
            pl.when(inside(d))(copy.start)

        return copy

    def straight(src, dst_of, d):
        copy = remote(src, dst_of(FAR[d]), (me + 2 * d * spacing, hd), inside(2 * d))
        pl.when(inside(2 * d))(copy.start)
        return copy

    def near_arrived(first, d):
        pl.when(inside(-d))(first.wait_recv)

    def arrived(second, d):
        pl.when(inside(-2 * d))(second.wait_recv)

    def rows_of(buffer, h):
        return lambda index: buffer.at[h, slot(index)]

    def tile_of(buffer):
        return lambda index: buffer.at[index]

    both = (1, -1)
    k1 = {(h, d): first_step(k_hbm.at[:, cols(h)], rows_of(kb, h), d) for h in range(heads) for d in both}
    v1 = {(h, d): first_step(v_hbm.at[:, cols(h)], rows_of(vb, h), d, core != 1) for h in range(heads) for d in both}

    for d in both:
        for index, away in ((NEAR[d], -d), (FAR[d], -2 * d)):

            @pl.when(jnp.logical_not(inside(away)))
            def _():
                for buffer in (kb, vb, qb, ab):
                    for h in range(heads):
                        buffer[h, slot(index)] = jnp.zeros((D, D), BF16)
                st1[index] = jnp.zeros(st1.shape[1:], F32)
                st2[index] = jnp.zeros(st2.shape[1:], F32)

    for copy in local:
        copy.wait()
    allowed = {}
    for offset, column in COLUMN.items():
        allowed[offset] = inside(offset) & (on_ref[0, column] == 1)
    factor = {0: scaling}
    shift = {0: 0.0}
    for offset in COLUMN:
        factor[offset] = jnp.where(allowed[offset], scaling, 0.0).astype(F32)
        shift[offset] = jnp.where(allowed[offset], 0.0, NEG).astype(F32)


    def compute_scores(h, index):
        offset = SLOT_OFFSET[index]
        raw = nt(qb[h, slot(0)], kb[h, slot(index)])
        score[h, :, slot(index)] = raw * factor[offset] + shift[offset]

    for h in range(heads):
        compute_scores(h, 0)
    k2 = {}
    for h in range(heads):
        for d in both:
            k2[h, d] = second_step(k1[h, d], rows_of(kb, h), d)
        for d in both:
            compute_scores(h, NEAR[d])
    for h in range(heads):
        for d in both:
            pl.when(inside(d) & (core == 1))(v1[h, d].start)
    v2 = {}
    for h in range(heads):
        for d in both:
            v2[h, d] = second_step(v1[h, d], rows_of(vb, h), d)
    q1 = {(h, d): first_step(q_hbm.at[:, cols(h)], rows_of(qb, h), d, core != 1) for h in range(heads) for d in both}

    lane = lax.broadcasted_iota(jnp.int32, (D, D), 1)

    def as_rows(columns):
        packed = jnp.zeros((D, D), F32)
        for i, column in enumerate(columns):
            packed = jnp.where(lane == i, column, packed)
        return packed.T

    peaks, inverses = [], []
    for h in range(heads):
        for d in both:
            arrived(k2[h, d], d)
        for d in both:
            compute_scores(h, FAR[d])
        pieces = [score[h, :, slot(i)] for i in range(5)]
        top = functools.reduce(jnp.maximum, pieces)
        peak = jnp.max(top, axis=1, keepdims=True)
        exponents = [jnp.exp(piece - peak) for piece in pieces]
        total = jnp.sum(functools.reduce(jnp.add, exponents), axis=1, keepdims=True)
        inverse_total = 1.0 / total
        for i in range(5):
            weight = exponents[i] * inverse_total
            score[h, :, slot(i)] = weight
            probs[h, :, slot(i)] = weight.astype(BF16)
        peaks.append(peak)
        inverses.append(inverse_total)
    for h in range(heads):
        for d in both:
            pl.when(inside(d) & (core == 1))(q1[h, d].start)
    st1[0] = as_rows(peaks + inverses + [-shift[offset] for offset in COLUMN])[0:16]
    s1 = {d: first_step(st1.at[0], tile_of(st1), d) for d in both}
    s2 = {d: straight(st1.at[0], tile_of(st1), d) for d in both}

    near_rows = 3 * D
    partial = [nn(probs[h, :, 0:near_rows], vb[h, 0:near_rows]) for h in range(heads)]
    sums_g, sums_a = [], []
    for h in range(heads):
        for d in both:
            arrived(v2[h, d], d)
        value = partial[h] + nn(probs[h, :, near_rows:], vb[h, near_rows:])
        attn[h] = value.astype(BF16)
        wide = attn[h].astype(F32)
        gradient = dob[h].astype(F32) * gain_ref[cols(h)][None, :]
        sums_g.append(jnp.sum(gradient * wide, axis=1, keepdims=True))
        sums_a.append(jnp.sum(wide * wide, axis=1, keepdims=True))
    sums[0] = as_rows([functools.reduce(jnp.add, sums_g), functools.reduce(jnp.add, sums_a)])[0:8]
    exchanged = []
    for p in range(1, peers):
        copy = remote(sums.at[0], sums.at[p], (me, lax.rem(hd + p, peers)), True)
        copy.start()
        exchanged.append(copy)

    for d in both:
        near_arrived(s1[d], d)
    q2 = {}
    for h in range(heads):
        for d in both:
            q2[h, d] = second_step(q1[h, d], rows_of(qb, h), d)

    def weights_back(h, index):
        offset = SLOT_OFFSET[index]
        peak = st1[index, h : h + 1]
        if offset:
            row = 2 * heads + COLUMN[-offset]
            peak = peak + st1[index, row : row + 1]
        raw = nt(kb[h, slot(0)], qb[h, slot(index)]) * scaling
        weight = jnp.exp(raw - peak) * st1[index, heads + h : heads + h + 1]
        score_t[h, :, slot(index)] = weight
        probs_t[h, :, slot(index)] = weight.astype(BF16)

    for h in range(heads):
        for index in range(3):
            weights_back(h, index)

    for copy in exchanged:
        copy.wait_recv()
    all_rows = functools.reduce(jnp.add, [sums[p] for p in range(peers)])
    along = all_rows[0:1]
    square = all_rows[1:2]
    inverse = lax.rsqrt(square / full_width + EPS)
    coefficient = inverse * inverse * inverse * along / full_width
    sublane = lax.broadcasted_iota(jnp.int32, (D, D), 0)
    columns = jnp.where(sublane == 0, inverse, coefficient).T
    inverse_col = columns[:, 0:1]
    coefficient_col = columns[:, 1:2]
    a1 = {}
    for h in range(heads):
        gradient = dob[h].astype(F32) * gain_ref[cols(h)][None, :]
        wide = attn[h].astype(F32)
        ab[h, slot(0)] = (inverse_col * gradient - wide * coefficient_col).astype(BF16)
        for d in both:
            a1[h, d] = first_step(ab.at[h, slot(0)], rows_of(ab, h), d)
    deltas = [
        jnp.sum(ab[h, slot(0)].astype(F32) * attn[h].astype(F32), axis=1, keepdims=True) for h in range(heads)
    ]
    st2[0] = as_rows(deltas)[0:8]
    e1 = {d: first_step(st2.at[0], tile_of(st2), d) for d in both}
    e2 = {d: straight(st2.at[0], tile_of(st2), d) for d in both}
    a2 = {(heads - 1, d): straight(ab.at[heads - 1, slot(0)], rows_of(ab, heads - 1), d) for d in both}
    for h in range(heads):
        out_ref[:, cols(h)] = (attn[h].astype(F32) * inverse_col * gain_ref[cols(h)][None, :]).astype(BF16)

    def query_gradient(h):
        d_weights = nt(ab[h, slot(0)], vb[h])
        d_score = (score[h] * (d_weights - deltas[h])).astype(BF16)
        dq_ref[:, cols(h)] = (nn(d_score, kb[h]) * scaling).astype(BF16)

    def key_gradients(h, low, high):
        rows = slice(low * D, high * D)
        delta = jnp.concatenate([st2[i, h : h + 1] for i in range(low, high)], axis=1)
        value_part = nn(probs_t[h, :, rows], ab[h, rows])
        d_weights = nt(vb[h, slot(0)], ab[h, rows])
        d_score = (score_t[h, :, rows] * (d_weights - delta)).astype(BF16)
        return nn(d_score, qb[h, rows]), value_part

    for h in range(heads):
        query_gradient(h)
    for h in range(heads):
        dk_acc[h], dv_acc[h] = key_gradients(h, 0, 1)
    for d in both:
        arrived(s2[d], d)
    for h in range(heads):
        for d in both:
            arrived(q2[h, d], d)
        for d in both:
            weights_back(h, FAR[d])
    for h in range(heads - 1):
        for d in both:
            a2[h, d] = second_step(a1[h, d], rows_of(ab, h), d)
    for d in both:
        near_arrived(a1[heads - 1, d], d)
        near_arrived(e1[d], d)
    for h in range(heads):
        key_part, value_part = key_gradients(h, 1, 3)
        dk_acc[h] += key_part
        dv_acc[h] += value_part
    for d in both:
        arrived(e2[d], d)
    for h in range(heads):
        for d in both:
            arrived(a2[h, d], d)
        key_part, value_part = key_gradients(h, 3, 5)
        dk_ref[:, cols(h)] = ((dk_acc[h] + key_part) * scaling).astype(BF16)
        dv_ref[:, cols(h)] = (dv_acc[h] + value_part).astype(BF16)
    for copy, condition in sent:
        if condition is True:
            copy.wait_send()
        else:
            pl.when(condition)(copy.wait_send)


def hand_on(*refs):
    *refs, sem = refs
    copies = []
    for i, (src, dst) in enumerate(zip(refs[: len(refs) // 2], refs[len(refs) // 2 :])):
        copies.append(pltpu.make_async_copy(src, dst, sem.at[i]))
        copies[-1].start()
    for copy in copies:
        copy.wait()


def local(queries, keys, values, d_out, gain, blocks_on):
    rows, width = queries.shape
    heads = width // D
    spacing = lax.axis_size("band") // 8
    peers = lax.axis_size("head")
    block = jax.ShapeDtypeStruct((rows, width), BF16)
    anywhere = pl.BlockSpec(memory_space=pl.ANY)
    vmem = pl.BlockSpec(memory_space=pltpu.VMEM)
    copies = 2 * 2 * 4 * heads + 8 + peers - 1
    results = pl.pallas_call(
        functools.partial(kernel, heads, spacing, 8, peers),
        out_shape=[block] * 4,
        in_specs=[anywhere] * 6,
        out_specs=[vmem] * 4,
        scratch_shapes=[pltpu.VMEM((heads, 5 * D, D), BF16)] * 4
        + [
            pltpu.VMEM((heads, D, D), BF16),
            pltpu.VMEM((width,), F32),
            pltpu.SMEM((1, 4), jnp.int32),
            pltpu.VMEM((heads, D, D), BF16),
            pltpu.VMEM((heads, D, 5 * D), F32),
            pltpu.VMEM((heads, D, 5 * D), BF16),
            pltpu.VMEM((heads, D, 5 * D), F32),
            pltpu.VMEM((heads, D, 5 * D), BF16),
            pltpu.VMEM((heads, D, D), F32),
            pltpu.VMEM((heads, D, D), F32),
            pltpu.VMEM((5, 16, D), F32),
            pltpu.VMEM((5, 8, D), F32),
            pltpu.VMEM((peers, 8, D), F32),
            pltpu.SemaphoreType.DMA((copies,)),
            pltpu.SemaphoreType.DMA((copies,)),
            pltpu.SemaphoreType.DMA((4 * heads + 2,)),
        ],
        compiler_params=pltpu.CompilerParams(
            collective_id=0, has_side_effects=True, vmem_limit_bytes=VMEM
        ),
        cost_estimate=pl.CostEstimate(flops=505_000_000, bytes_accessed=800_000, transcendentals=500_000),
        name="attention",
    )(*[pltpu.with_memory_space_constraint(x, pltpu.HBM) for x in (queries, keys, values, d_out, gain, blocks_on)])
    passed = pl.pallas_call(
        hand_on,
        out_shape=[block] * 4,
        in_specs=[vmem] * 4,
        out_specs=[anywhere] * 4,
        scratch_shapes=[pltpu.SemaphoreType.DMA((4,))],
        compiler_params=pltpu.CompilerParams(vmem_limit_bytes=8 * 1024 * 1024),
        name="hand_on",
    )(*results)
    return tuple(passed)


def solution(mesh):
    in_specs = (
        P("band", "head"),
        P("band", "head"),
        P("band", "head"),
        P("band", "head"),
        P("head"),
        P("band", None),
    )
    out_specs = (P("band", "head"), P("band", "head"), P("band", "head"), P("band", "head"))
    return jax.shard_map(local, mesh=mesh, in_specs=in_specs, out_specs=out_specs, check_vma=False)
```

```python
import functools

import jax
import jax.numpy as jnp
from jax import lax
from jax.experimental import pallas as pl
from jax.experimental.pallas import tpu as pltpu
from jax.sharding import PartitionSpec as P

D = 128
NEG = -1e30
EPS = 1e-06
VMEM = 32 * 1024 * 1024
MESH = pl.DeviceIdType.MESH
BF16 = jnp.bfloat16
F32 = jnp.float32

SLOT_OFFSET = (0, -1, 1, -2, 2)
COLUMN = {-2: 0, -1: 1, 1: 2, 2: 3}
NEAR = {1: 1, -1: 2}
FAR = {1: 3, -1: 4}


def nt(left, right):
    return lax.dot_general(left, right, (((1,), (1,)), ((), ())), preferred_element_type=F32)


def nn(left, right):
    return jnp.dot(left, right, preferred_element_type=F32)


def kernel(
    heads,
    spacing,
    steps,
    peers,
    q_hbm,
    k_hbm,
    v_hbm,
    do_hbm,
    gain_hbm,
    on_hbm,
    out_ref,
    dq_ref,
    dk_ref,
    dv_ref,
    kb,
    vb,
    qb,
    ab,
    dob,
    gain_ref,
    on_ref,
    grad,
    attn,
    score,
    probs,
    score_t,
    probs_t,
    dk_acc,
    dv_acc,
    st1,
    st2,
    sums,
    send_sem,
    recv_sem,
    local_sem,
):
    me = lax.axis_index("band")
    hd = lax.axis_index("head")
    z = me // spacing
    core = lax.rem(me, 2)
    width = heads * D
    full_width = width * peers
    scaling = D ** (-0.5)

    def inside(offset):
        return (z + offset >= 0) & (z + offset < steps)

    def slot(index):
        return pl.ds(index * D, D)

    def cols(h):
        return slice(h * D, (h + 1) * D)

    barrier = pltpu.get_barrier_semaphore()
    expected = jnp.int32(peers - 1)
    for d in COLUMN:

        @pl.when(inside(d))
        def _():
            pl.semaphore_signal(barrier, 1, device_id=(me + d * spacing, hd), device_id_type=MESH)

        expected = expected + inside(d).astype(jnp.int32)
    for p in range(1, peers):
        pl.semaphore_signal(barrier, 1, device_id=(me, lax.rem(hd + p, peers)), device_id_type=MESH)
    local = []

    def fetch(src, dst):
        copy = pltpu.make_async_copy(src, dst, local_sem.at[len(local)])
        copy.start()
        local.append(copy)

    fetch(on_hbm, on_ref)
    for h in range(heads):
        fetch(q_hbm.at[:, cols(h)], qb.at[h, slot(0)])
        fetch(k_hbm.at[:, cols(h)], kb.at[h, slot(0)])
    for h in range(heads):
        fetch(v_hbm.at[:, cols(h)], vb.at[h, slot(0)])
    fetch(gain_hbm, gain_ref)
    for h in range(heads):
        fetch(do_hbm.at[:, cols(h)], dob.at[h])

    pl.semaphore_wait(barrier, expected)

    used = [0]
    sent = []

    def remote(src, dst, device, condition):
        index = used[0]
        used[0] += 1
        copy = pltpu.make_async_remote_copy(
            src, dst, send_sem.at[index], recv_sem.at[index], device_id=device, device_id_type=MESH
        )
        sent.append((copy, condition))
        return copy

    def first_step(src, dst_of, d, also=True):
        copy = remote(src, dst_of(NEAR[d]), (me + d * spacing, hd), inside(d))
        pl.when(inside(d) & also)(copy.start)
        return copy

    def second_step(first, dst_of, d):
        copy = remote(dst_of(NEAR[d]), dst_of(FAR[d]), (me + d * spacing, hd), inside(d) & inside(-d))

        @pl.when(inside(-d))
        def _():
            first.wait_recv()
            pl.when(inside(d))(copy.start)

        return copy

    def straight(src, dst_of, d):
        copy = remote(src, dst_of(FAR[d]), (me + 2 * d * spacing, hd), inside(2 * d))
        pl.when(inside(2 * d))(copy.start)
        return copy

    def near_arrived(first, d):
        pl.when(inside(-d))(first.wait_recv)

    def arrived(second, d):
        pl.when(inside(-2 * d))(second.wait_recv)

    def rows_of(buffer, h):
        return lambda index: buffer.at[h, slot(index)]

    def tile_of(buffer):
        return lambda index: buffer.at[index]

    both = (1, -1)
    k1 = {(h, d): first_step(k_hbm.at[:, cols(h)], rows_of(kb, h), d) for h in range(heads) for d in both}
    v1 = {(h, d): first_step(v_hbm.at[:, cols(h)], rows_of(vb, h), d, core != 1) for h in range(heads) for d in both}

    for d in both:
        for index, away in ((NEAR[d], -d), (FAR[d], -2 * d)):

            @pl.when(jnp.logical_not(inside(away)))
            def _():
                for buffer in (kb, vb, qb, ab):
                    for h in range(heads):
                        buffer[h, slot(index)] = jnp.zeros((D, D), BF16)
                st1[index] = jnp.zeros(st1.shape[1:], F32)
                st2[index] = jnp.zeros(st2.shape[1:], F32)

    for copy in local:
        copy.wait()
    allowed = {}
    for offset, column in COLUMN.items():
        allowed[offset] = inside(offset) & (on_ref[0, column] == 1)
    factor = {0: scaling}
    shift = {0: 0.0}
    for offset in COLUMN:
        factor[offset] = jnp.where(allowed[offset], scaling, 0.0).astype(F32)
        shift[offset] = jnp.where(allowed[offset], 0.0, NEG).astype(F32)


    def compute_scores(h, index):
        offset = SLOT_OFFSET[index]
        raw = nt(qb[h, slot(0)], kb[h, slot(index)])
        score[h, :, slot(index)] = raw * factor[offset] + shift[offset]

    for h in range(heads):
        compute_scores(h, 0)
    k2 = {}
    for h in range(heads):
        for d in both:
            k2[h, d] = second_step(k1[h, d], rows_of(kb, h), d)
        for d in both:
            compute_scores(h, NEAR[d])
    for h in range(heads):
        for d in both:
            pl.when(inside(d) & (core == 1))(v1[h, d].start)
    v2 = {}
    for h in range(heads):
        for d in both:
            v2[h, d] = second_step(v1[h, d], rows_of(vb, h), d)
    q1 = {(h, d): first_step(q_hbm.at[:, cols(h)], rows_of(qb, h), d, core != 1) for h in range(heads) for d in both}

    sums[0] = jnp.zeros(sums.shape[1:], F32)
    lane = lax.broadcasted_iota(jnp.int32, (D, D), 1)

    def as_rows(columns):
        packed = jnp.zeros((D, D), F32)
        for i, column in enumerate(columns):
            packed = jnp.where(lane == i, column, packed)
        return packed.T

    peaks, inverses = [], []
    for h in range(heads):
        for d in both:
            arrived(k2[h, d], d)
        for d in both:
            compute_scores(h, FAR[d])
        pieces = [score[h, :, slot(i)] for i in range(5)]
        top = functools.reduce(jnp.maximum, pieces)
        peak = jnp.max(top, axis=1, keepdims=True)
        exponents = [jnp.exp(piece - peak) for piece in pieces]
        total = jnp.sum(functools.reduce(jnp.add, exponents), axis=1, keepdims=True)
        inverse_total = 1.0 / total
        for i in range(5):
            weight = exponents[i] * inverse_total
            score[h, :, slot(i)] = weight
            probs[h, :, slot(i)] = weight.astype(BF16)
        peaks.append(peak)
        inverses.append(inverse_total)
    st1[0] = as_rows(peaks + inverses + [-shift[offset] for offset in COLUMN])[0:16]
    s1 = {d: first_step(st1.at[0], tile_of(st1), d) for d in both}
    s2 = {d: straight(st1.at[0], tile_of(st1), d) for d in both}

    near_rows = 3 * D
    for h in range(heads):
        for d in both:
            pl.when(inside(d) & (core == 1))(q1[h, d].start)
    partial = [nn(probs[h, :, 0:near_rows], vb[h, 0:near_rows]) for h in range(heads)]
    for h in range(heads):
        grad[h] = dob[h].astype(F32) * gain_ref[cols(h)][None, :]
    sum_g = jnp.zeros((D, D), F32)
    sum_a = jnp.zeros((D, D), F32)
    for h in range(heads):
        for d in both:
            arrived(v2[h, d], d)
        value = partial[h] + nn(probs[h, :, near_rows:], vb[h, near_rows:])
        attn[h] = value.astype(BF16)
        wide = attn[h].astype(F32)
        sum_g += grad[h] * wide
        sum_a += wide * wide
    sums[0, 0:1] = jnp.sum(sum_g.T, axis=0, keepdims=True)
    sums[0, 1:2] = jnp.sum(sum_a.T, axis=0, keepdims=True)
    exchanged = []
    for p in range(1, peers):
        copy = remote(sums.at[0], sums.at[p], (me, lax.rem(hd + p, peers)), True)
        copy.start()
        exchanged.append(copy)

    for d in both:
        near_arrived(s1[d], d)
    q2 = {}
    for h in range(heads):
        for d in both:
            q2[h, d] = second_step(q1[h, d], rows_of(qb, h), d)

    def weights_back(h, index):
        offset = SLOT_OFFSET[index]
        peak = st1[index, h : h + 1]
        if offset:
            row = 2 * heads + COLUMN[-offset]
            peak = peak + st1[index, row : row + 1]
        raw = nt(kb[h, slot(0)], qb[h, slot(index)]) * scaling
        weight = jnp.exp(raw - peak) * st1[index, heads + h : heads + h + 1]
        score_t[h, :, slot(index)] = weight
        probs_t[h, :, slot(index)] = weight.astype(BF16)

    for h in range(heads):
        for index in range(3):
            weights_back(h, index)

    for copy in exchanged:
        copy.wait_recv()
    all_rows = functools.reduce(jnp.add, [sums[p] for p in range(peers)])
    along = all_rows[0:1]
    square = all_rows[1:2]
    inverse = lax.rsqrt(square / full_width + EPS)
    coefficient = inverse * inverse * inverse * along / full_width
    sublane = lax.broadcasted_iota(jnp.int32, (D, D), 0)
    columns = jnp.where(sublane == 0, inverse, coefficient).T
    inverse_col = columns[:, 0:1]
    coefficient_col = columns[:, 1:2]
    a1 = {}
    for h in range(heads):
        gradient = grad[h]
        wide = attn[h].astype(F32)
        ab[h, slot(0)] = (inverse_col * gradient - wide * coefficient_col).astype(BF16)
        for d in both:
            a1[h, d] = first_step(ab.at[h, slot(0)], rows_of(ab, h), d)
    deltas = [
        jnp.sum(ab[h, slot(0)].astype(F32) * attn[h].astype(F32), axis=1, keepdims=True) for h in range(heads)
    ]
    st2[0] = as_rows(deltas)[0:8]
    e1 = {d: first_step(st2.at[0], tile_of(st2), d) for d in both}
    e2 = {d: straight(st2.at[0], tile_of(st2), d) for d in both}
    a2 = {}
    for h in range(heads):
        out_ref[:, cols(h)] = (attn[h].astype(F32) * inverse_col * gain_ref[cols(h)][None, :]).astype(BF16)

    def query_gradient(h):
        d_weights = nt(ab[h, slot(0)], vb[h])
        d_score = (score[h] * (d_weights - deltas[h])).astype(BF16)
        dq_ref[:, cols(h)] = (nn(d_score, kb[h]) * scaling).astype(BF16)

    def key_gradients(h, low, high):
        rows = slice(low * D, high * D)
        delta = jnp.concatenate([st2[i, h : h + 1] for i in range(low, high)], axis=1)
        value_part = nn(probs_t[h, :, rows], ab[h, rows])
        d_weights = nt(vb[h, slot(0)], ab[h, rows])
        d_score = (score_t[h, :, rows] * (d_weights - delta)).astype(BF16)
        return nn(d_score, qb[h, rows]), value_part

    for h in range(heads):
        query_gradient(h)
    for h in range(heads):
        dk_acc[h], dv_acc[h] = key_gradients(h, 0, 1)
    for d in both:
        arrived(s2[d], d)
    for h in range(heads):
        for d in both:
            arrived(q2[h, d], d)
        for d in both:
            weights_back(h, FAR[d])
    for h in range(heads):
        for d in both:
            a2[h, d] = second_step(a1[h, d], rows_of(ab, h), d)
    for d in both:
        near_arrived(e1[d], d)
    for h in range(heads):
        key_part, value_part = key_gradients(h, 1, 3)
        dk_acc[h] += key_part
        dv_acc[h] += value_part
    for d in both:
        arrived(e2[d], d)
    for h in range(heads):
        for d in both:
            arrived(a2[h, d], d)
        key_part, value_part = key_gradients(h, 3, 5)
        dk_ref[:, cols(h)] = ((dk_acc[h] + key_part) * scaling).astype(BF16)
        dv_ref[:, cols(h)] = (dv_acc[h] + value_part).astype(BF16)
    for copy, condition in sent:
        if condition is True:
            copy.wait_send()
        else:
            pl.when(condition)(copy.wait_send)


def hand_on(*refs):
    *refs, sem = refs
    copies = []
    for i, (src, dst) in enumerate(zip(refs[: len(refs) // 2], refs[len(refs) // 2 :])):
        copies.append(pltpu.make_async_copy(src, dst, sem.at[i]))
        copies[-1].start()
    for copy in copies:
        copy.wait()


def local(queries, keys, values, d_out, gain, blocks_on):
    rows, width = queries.shape
    heads = width // D
    spacing = lax.axis_size("band") // 8
    peers = lax.axis_size("head")
    block = jax.ShapeDtypeStruct((rows, width), BF16)
    anywhere = pl.BlockSpec(memory_space=pl.ANY)
    vmem = pl.BlockSpec(memory_space=pltpu.VMEM)
    copies = 2 * 2 * 4 * heads + 8 + peers - 1
    results = pl.pallas_call(
        functools.partial(kernel, heads, spacing, 8, peers),
        out_shape=[block] * 4,
        in_specs=[anywhere] * 6,
        out_specs=[vmem] * 4,
        scratch_shapes=[pltpu.VMEM((heads, 5 * D, D), BF16)] * 4
        + [
            pltpu.VMEM((heads, D, D), BF16),
            pltpu.VMEM((width,), F32),
            pltpu.SMEM((1, 4), jnp.int32),
            pltpu.VMEM((heads, D, D), F32),
            pltpu.VMEM((heads, D, D), BF16),
            pltpu.VMEM((heads, D, 5 * D), F32),
            pltpu.VMEM((heads, D, 5 * D), BF16),
            pltpu.VMEM((heads, D, 5 * D), F32),
            pltpu.VMEM((heads, D, 5 * D), BF16),
            pltpu.VMEM((heads, D, D), F32),
            pltpu.VMEM((heads, D, D), F32),
            pltpu.VMEM((5, 16, D), F32),
            pltpu.VMEM((5, 8, D), F32),
            pltpu.VMEM((peers, 8, D), F32),
            pltpu.SemaphoreType.DMA((copies,)),
            pltpu.SemaphoreType.DMA((copies,)),
            pltpu.SemaphoreType.DMA((4 * heads + 2,)),
        ],
        compiler_params=pltpu.CompilerParams(
            collective_id=0, has_side_effects=True, vmem_limit_bytes=VMEM
        ),
        cost_estimate=pl.CostEstimate(flops=505_000_000, bytes_accessed=800_000, transcendentals=500_000),
        name="attention",
    )(*[pltpu.with_memory_space_constraint(x, pltpu.HBM) for x in (queries, keys, values, d_out, gain, blocks_on)])
    passed = pl.pallas_call(
        hand_on,
        out_shape=[block] * 4,
        in_specs=[vmem] * 4,
        out_specs=[anywhere] * 4,
        scratch_shapes=[pltpu.SemaphoreType.DMA((4,))],
        compiler_params=pltpu.CompilerParams(vmem_limit_bytes=8 * 1024 * 1024),
        name="hand_on",
    )(*results)
    return tuple(passed)


def solution(mesh):
    in_specs = (
        P("band", "head"),
        P("band", "head"),
        P("band", "head"),
        P("band", "head"),
        P("head"),
        P("band", None),
    )
    out_specs = (P("band", "head"), P("band", "head"), P("band", "head"), P("band", "head"))
    return jax.shard_map(local, mesh=mesh, in_specs=in_specs, out_specs=out_specs, check_vma=False)
```
